128 devices in a mesh: gx: 8 (over y, core), gy: 16 (over z, x).
Axes of the slice: x: 4, y: 4, z: 4, core: 2. Of those that a mesh axis runs over, the one named last changes fastest.
Arguments:
- hidden: bfloat16 [16384, 512], P(('gx', 'gy')), may hold values from -16 to 16
- queries: bfloat16 [512, 8192], P('gx', 'gy'), may hold values from -8 to 8
- new_kv: bfloat16 [512, 1024], P('gx', 'gy'), may hold values from -6 to 6
- key_cache: bfloat16 [512, 256, 512], P(('gx', 'gy')), may hold values from -8 to 8
- value_cache: bfloat16 [512, 256, 512], P(('gx', 'gy')), may hold values from -8 to 8
- lengths: int32 [512], P(('gx', 'gy')), may hold values from 2 to 256, as said below
- out_weight: bfloat16 [8192, 16384], P('gy', 'gx'), may hold values from -0.0625 to 0.0625
- norm_gain: bfloat16 [16384], P(('gx', 'gy')), may hold values from 0.099609375 to 1.8984375
- w_gate: bfloat16 [16384, 26624], P('gx', 'gy'), may hold values from -0.046875 to 0.046875
- w_up: bfloat16 [16384, 26624], P('gx', 'gy'), may hold values from -0.046875 to 0.046875
- w_down: bfloat16 [26624, 16384], P('gy', 'gx'), may hold values from -0.0390625 to 0.0390625
Outputs:
- mixed: bfloat16 [16384, 512], P(('gx', 'gy'))
The draws below stay inside these ranges and needn't reach their ends.
Inputs may be any that keep to these rules, and one draw needn't show every extreme that they name: `lengths`: every beam row has 2 or more live positions; some beam row has all 256.
All inputs are finite; a program needn't handle non-finite values.
Results may differ from the reference program's by a relative error of at most 0.019.
Values may be sent and summed in bfloat16 or wider, within the bound.
No kernel may reach another device: no remote copies, remote signals or barrier semaphores. Data moves between devices by JAX's collectives and lax.ppermute only.
A program may use at most 128 MiB of HBM per device.

```python
import jax
import jax.numpy as jnp
from jax import lax

D = 16384
FF = 26624
HQ = 64
HK = 4
HD = 128
CACHE = 256
BEAMS = 512


def draw_hidden(key, part):
    key = jax.random.fold_in(key, 11)
    leading_key, second_key, third_key = jax.random.split(key, 3)
    ramp = jnp.arange(D, dtype=jnp.float32) / D - 0.5
    feature_scale = jnp.exp(0.5 * jnp.log(3.0) * ramp) * jnp.exp(jax.random.uniform(second_key, (D,), jnp.float32, jnp.log(0.5), jnp.log(2.0)))
    base = jnp.clip(jax.random.normal(leading_key, (D, BEAMS), jnp.float32), -6.0, 6.0)
    beam_scale = jnp.exp(jax.random.uniform(third_key, (BEAMS,), jnp.float32, jnp.log(0.5), jnp.log(2.0)))
    values = jnp.clip(base * feature_scale[:, None] * beam_scale[None, :], -16.0, 16.0)
    return values.astype(jnp.bfloat16)


def draw_queries(key, part):
    key = jax.random.fold_in(key, 3)
    grouped = HQ // HK
    values = jnp.clip(jax.random.normal(key, (BEAMS, HK, grouped, HD), jnp.float32), -4.0, 4.0)
    return values.reshape(BEAMS, HQ * HD).astype(jnp.bfloat16)


def draw_key_cache(key, part):
    key = jax.random.fold_in(key, 5)
    values = jnp.clip(jax.random.normal(key, (BEAMS, CACHE, HK * HD), jnp.float32), -4.0, 4.0)
    return values.astype(jnp.bfloat16)


def draw_lengths(key, part):
    key = jax.random.fold_in(key, 7)
    leading_key, second_key = jax.random.split(key)
    counts = jax.random.randint(leading_key, (BEAMS,), 2, CACHE + 1)
    full_row = jax.random.randint(second_key, (), 0, BEAMS)
    return counts.at[full_row].set(CACHE).astype(jnp.int32)


def block_levels(own_key, dims, cuts, smallest, top_value):
    gain, own = 1.0, jax.random.fold_in(own_key, 6)
    for dim, shards_of in cuts:
        heights = jnp.exp(jax.random.uniform(jax.random.fold_in(own, dim), (shards_of,), jnp.float32, smallest / len(cuts), top_value / len(cuts)))
        gain = gain * jnp.repeat(heights, dims[dim] // shards_of).reshape([-1 if axis == dim else 1 for axis in range(len(dims))])
    return gain


def normal_values(own_key, extent, deviation, reach, shards=(), held_as=jnp.bfloat16):
    drawn = deviation * jax.random.normal(own_key, extent, jnp.float32)
    if shards:
        drawn = drawn * block_levels(own_key, extent, shards, -0.22, 0.18)
    return jnp.clip(drawn, -reach, reach).astype(held_as)


def setup_inputs(seed: int = 0) -> dict:
    key_list = jax.random.split(jax.random.key(seed), 12)
    hidden = draw_hidden(jax.random.fold_in(key_list[11], 71), 0)
    queries = draw_queries(jax.random.fold_in(key_list[11], 71), 0)
    new_kv = normal_values(key_list[2], (BEAMS, 2 * HK * HD), 1.0, 6.0, ((0, 8), (1, 16)))
    key_cache = draw_key_cache(jax.random.fold_in(key_list[11], 71), 0)
    value_cache = normal_values(key_list[4], (BEAMS, CACHE, HK * HD), 2.0, 8.0, ((0, 128),))
    lengths = draw_lengths(jax.random.fold_in(key_list[11], 71), 0)
    out_weight = normal_values(key_list[6], (HQ * HD, D), (HQ * HD) ** -0.5, 0.0625, ((0, 16), (1, 8)))
    norm_gain = jnp.clip(1.0 + 0.18 * jax.random.normal(key_list[7], (D,), jnp.float32), 0.099609375, 1.8984375).astype(jnp.bfloat16)
    w_gate = normal_values(key_list[8], (D, FF), D ** -0.5, 0.046875, ((0, 8), (1, 16)))
    w_up = normal_values(key_list[9], (D, FF), D ** -0.5, 0.046875, ((0, 8), (1, 16)))
    w_down = normal_values(key_list[10], (FF, D), FF ** -0.5, 0.0390625, ((0, 16), (1, 8)))
    return dict(hidden=hidden, queries=queries, new_kv=new_kv, key_cache=key_cache, value_cache=value_cache, lengths=lengths, out_weight=out_weight, norm_gain=norm_gain, w_gate=w_gate, w_up=w_up, w_down=w_down)


def wide_dot(left, right):
    return jnp.dot(left.astype(jnp.float32), right.astype(jnp.float32), precision=lax.Precision.HIGHEST)

def reference(hidden, queries, new_kv, key_cache, value_cache, lengths, out_weight, norm_gain, w_gate, w_up, w_down):
    grouped = HQ // HK
    score_scale = 1.0 / HD ** 0.5
    query_vector = queries.astype(jnp.float32).reshape(BEAMS, HK, grouped, HD)
    keys_all = key_cache.astype(jnp.float32).reshape(BEAMS, CACHE, HK, HD)
    values_all = value_cache.astype(jnp.float32).reshape(BEAMS, CACHE, HK, HD)
    pair = new_kv.astype(jnp.float32)
    fresh_key = pair[:, :HK * HD].reshape(BEAMS, HK, HD)
    new_value = pair[:, HK * HD:].reshape(BEAMS, HK, HD)
    scores = jnp.einsum('bkgd,blkd->bkgl', query_vector, keys_all, precision=lax.Precision.HIGHEST) * score_scale
    live_mask = jnp.arange(CACHE)[None, :] < lengths[:, None]
    scores = jnp.where(live_mask[:, None, None, :], scores, -jnp.inf)
    self_score = jnp.einsum('qytz,qyz->qyt', query_vector, fresh_key, precision=lax.Precision.HIGHEST) * score_scale
    peak = jnp.maximum(lax.optimization_barrier(jnp.max(scores, axis=-1)), self_score)
    raw_weights = jnp.exp(scores - peak[..., None])
    self_weight = jnp.exp(self_score - peak)
    total = lax.optimization_barrier(jnp.sum(raw_weights, axis=-1)) + self_weight
    probs = (raw_weights / total[..., None]).astype(jnp.bfloat16)
    own_prob = (self_weight / total).astype(jnp.bfloat16)
    attended = jnp.einsum('bkgl,blkd->bkgd', probs.astype(jnp.float32), values_all, precision=lax.Precision.HIGHEST)
    attended = attended + own_prob.astype(jnp.float32)[..., None] * new_value[:, :, None, :]
    attended = attended.astype(jnp.bfloat16).reshape(BEAMS, HQ * HD)
    attention_result = wide_dot(attended, out_weight).T
    resid = (hidden.astype(jnp.float32) + attention_result).astype(jnp.bfloat16)
    resid_wide = resid.astype(jnp.float32)
    squares = lax.optimization_barrier(jnp.sum(resid_wide * resid_wide, axis=0))
    normed = (resid_wide * lax.rsqrt(squares / D + 1e-05)[None, :] * norm_gain.astype(jnp.float32)[:, None]).astype(jnp.bfloat16)
    gate = wide_dot(w_gate.T, normed)
    up_part = wide_dot(w_up.T, normed)
    act = (jax.nn.silu(gate) * up_part).astype(jnp.bfloat16)
    down = wide_dot(w_down.T, act)
    return (resid_wide + down).astype(jnp.bfloat16)
```

```python
import jax
import jax.numpy as jnp
from jax import lax
from jax.sharding import PartitionSpec as P

D = 16384
HQ = 64
HK = 4
HD = 128
bf16 = jnp.bfloat16
f32 = jnp.float32


def attend(query_rows, pair_rows, key_cache, value_cache, lengths):
    grouped = HQ // HK
    score_scale = 1.0 / HD**0.5
    beam_count = query_rows.shape[0]
    cache_len = key_cache.shape[1]
    query_vector = query_rows.reshape(beam_count, HK, grouped, HD)
    keys_all = key_cache.reshape(beam_count, cache_len, HK, HD)
    values_all = value_cache.reshape(beam_count, cache_len, HK, HD)
    fresh_key = pair_rows[:, : HK * HD].reshape(beam_count, HK, HD)
    new_value = pair_rows[:, HK * HD :].reshape(beam_count, HK, HD)
    scores = (
        jnp.einsum("bkgd,blkd->bkgl", query_vector, keys_all, preferred_element_type=f32)
        * score_scale
    )
    live_mask = jnp.arange(cache_len)[None, :] < lengths[:, None]
    scores = jnp.where(live_mask[:, None, None, :], scores, -jnp.inf)
    self_score = (
        jnp.einsum("qytz,qyz->qyt", query_vector, fresh_key, preferred_element_type=f32)
        * score_scale
    )
    peak = jnp.maximum(jnp.max(scores, axis=-1), self_score)
    raw_weights = jnp.exp(scores - peak[..., None])
    self_weight = jnp.exp(self_score - peak)
    total = jnp.sum(raw_weights, axis=-1) + self_weight
    probs = (raw_weights / total[..., None]).astype(bf16)
    own_prob = (self_weight / total).astype(bf16)
    attended = jnp.einsum("bkgl,blkd->bkgd", probs, values_all, preferred_element_type=f32)
    attended = (
        attended + own_prob.astype(f32)[..., None] * new_value.astype(f32)[:, :, None, :]
    )
    return attended.astype(bf16).reshape(beam_count, HQ * HD)


def from_x(a, d):
    return lax.ppermute(a, "gy", [(i, (i // 4) * 4 + (i % 4 - d) % 4) for i in range(16)])


def from_z(a, d):
    return lax.ppermute(a, "gy", [(i, ((i // 4 - d) % 4) * 4 + i % 4) for i in range(16)])


def from_y(a, d):
    return lax.ppermute(a, "gx", [(i, ((i // 2 - d) % 4) * 2 + i % 2) for i in range(8)])


def from_core(a):
    return lax.ppermute(a, "gx", [(i, i ^ 1) for i in range(8)])


def total_of(parts):
    out = parts[0].astype(f32)
    for part in parts[1:]:
        out = out + part.astype(f32)
    return out


def take_columns(a, block, width):
    return lax.dynamic_slice_in_dim(a, block * width, width, 1)


def absolute(parts, index):
    doubled = jnp.stack(list(parts) + list(parts[:3]))
    return lax.dynamic_slice_in_dim(doubled, (4 - index) % 4, 4, 0)


def scatter_gy(terms, z, x):
    half = terms.shape[0] // 2
    upper, lower = terms[:half], terms[half:]

    def x_group(k):
        place = (x + k) % 4
        return jnp.concatenate([take_columns(upper, zz * 4 + place, 128) for zz in range(4)], 1)

    def z_group(k):
        return take_columns(lower, (z + k) % 4, 512)

    upper_in, lower_in = [x_group(0)], [z_group(0)]
    for k in (2, 1, 3):
        upper_in.append(from_x(x_group(k), (4 - k) % 4))
        lower_in.append(from_z(z_group(k), (4 - k) % 4))
    upper_sum, lower_sum = total_of(upper_in).astype(bf16), total_of(lower_in).astype(bf16)
    upper_in, lower_in = [take_columns(upper_sum, z, 128)], [take_columns(lower_sum, x, 128)]
    for k in (2, 1, 3):
        upper_in.append(from_z(take_columns(upper_sum, (z + k) % 4, 128), (4 - k) % 4))
        lower_in.append(from_x(take_columns(lower_sum, (x + k) % 4, 128), (4 - k) % 4))
    return jnp.concatenate([total_of(upper_in), total_of(lower_in)], 0)


def gather_gy(rows, z, x):
    half = rows.shape[0] // 2
    upper, lower = rows[:half], rows[half:]
    upper = [upper] + [from_x(upper, k) for k in (1, 2, 3)]
    lower = [lower] + [from_z(lower, k) for k in (1, 2, 3)]
    upper, lower = absolute(upper, x), absolute(lower, z)
    upper = [upper] + [from_z(upper, k) for k in (1, 2, 3)]
    lower = [lower] + [from_x(lower, k) for k in (1, 2, 3)]
    upper, lower = absolute(upper, z), absolute(lower, x)
    upper = upper.transpose(2, 0, 1, 3).reshape(half, 2048)
    lower = lower.transpose(2, 1, 0, 3).reshape(half, 2048)
    return jnp.concatenate([upper, lower], 0)


def gather_gx(rows):
    same = jnp.concatenate([rows] + [from_y(rows, k) for k in (1, 2, 3)], 0)
    return jnp.concatenate([same, from_core(same)], 0)


def scatter_gx(terms):
    half = terms.shape[0] // 2
    same = (terms[:half].astype(f32) + from_core(terms[half:]).astype(f32)).astype(bf16)
    return total_of(
        [same[:64]] + [from_y(same[64 * k : 64 * k + 64], (4 - k) % 4) for k in (2, 1, 3)]
    )


def to_own_order(rows, y, core):
    blocks = rows.reshape(4, 2, 64, rows.shape[1])
    blocks = lax.dynamic_slice_in_dim(jnp.concatenate([blocks, blocks[:3]], 0), y, 4, 0)
    same = lax.dynamic_index_in_dim(blocks, core, 1, False)
    other = lax.dynamic_index_in_dim(blocks, 1 - core, 1, False)
    return jnp.concatenate([same, other], 0).reshape(rows.shape)


def from_own_order(rows, y, core):
    blocks = rows.reshape(2, 4, 64, rows.shape[1])
    blocks = lax.dynamic_slice_in_dim(
        jnp.concatenate([blocks, blocks[:, :3]], 1), (4 - y) % 4, 4, 1
    )
    first = lax.dynamic_index_in_dim(blocks, core, 0, False)
    second = lax.dynamic_index_in_dim(blocks, 1 - core, 0, False)
    return jnp.stack([first, second], 1).reshape(rows.shape)


def per_device(
    hidden,
    queries,
    new_kv,
    key_cache,
    value_cache,
    lengths,
    out_weight,
    norm_gain,
    w_gate,
    w_up,
    w_down,
):
    gx, gy = lax.axis_index("gx"), lax.axis_index("gy")
    y, core, z, x = gx // 2, gx % 2, gy // 4, gy % 4
    gain_rows = jnp.broadcast_to(norm_gain.reshape(1, 4, 32), (16, 4, 32)).reshape(64, 32)
    sent = jnp.concatenate([queries, new_kv, gain_rows], 1)
    got = lax.all_to_all(sent.reshape(16, 4, 608), "gy", 0, 0, tiled=True)
    query_rows = got[:, :, :512].transpose(1, 0, 2).reshape(4, 8192)
    pair_rows = got[:, :, 512:576].transpose(1, 0, 2).reshape(4, 1024)
    gain = got[:, :, 576:].reshape(1, 2048)
    attended = attend(query_rows, pair_rows, key_cache, value_cache, lengths)
    head_block = lax.all_to_all(attended, "gy", split_axis=1, concat_axis=0, tiled=True)
    heads = gather_gx(head_block)
    terms = jnp.dot(heads, out_weight, preferred_element_type=f32).astype(bf16)
    mine = to_own_order(hidden.T, y, core)
    resid = (mine.astype(f32) + scatter_gy(terms, z, x)).astype(bf16)
    features = gather_gy(resid, z, x).astype(f32)
    squares = jnp.sum(features * features, axis=1, keepdims=True)
    scaled = (features * gain.astype(f32)).astype(bf16)
    gate = jnp.dot(scaled, w_gate, preferred_element_type=f32).astype(bf16)
    up = jnp.dot(scaled, w_up, preferred_element_type=f32).astype(bf16)
    squares_wide = jnp.broadcast_to(squares, (512, 128))
    gate_sum = scatter_gx(gate)
    up_sum = scatter_gx(up)
    same = squares_wide[:256] + from_core(squares_wide[256:])
    square_sum = same[:64]
    for k in (2, 1, 3):
        square_sum = square_sum + from_y(same[64 * k : 64 * k + 64], (4 - k) % 4)
    scale = lax.rsqrt(square_sum[:, :1] / D + 1e-05)
    act = (jax.nn.silu(gate_sum * scale) * (up_sum * scale)).astype(bf16)
    down_terms = jnp.dot(gather_gx(act), w_down, preferred_element_type=f32).astype(bf16)
    mixed = (resid.astype(f32) + scatter_gy(down_terms, z, x)).astype(bf16)
    return from_own_order(mixed, y, core).T


def solution(mesh):
    return jax.shard_map(
        per_device,
        mesh=mesh,
        in_specs=(
            P(("gx", "gy"), None),
            P("gx", "gy"),
            P("gx", "gy"),
            P(("gx", "gy"), None, None),
            P(("gx", "gy"), None, None),
            P(("gx", "gy")),
            P("gy", "gx"),
            P(("gx", "gy")),
            P("gx", "gy"),
            P("gx", "gy"),
            P("gy", "gx"),
        ),
        out_specs=P(("gx", "gy"), None),
        check_vma=False,
    )
```

```python
import jax
import jax.numpy as jnp
from jax import lax
from jax.experimental import pallas as pl
from jax.experimental.pallas import tpu as pltpu
from jax.sharding import PartitionSpec as P

D = 16384
HQ = 64
HK = 4
HD = 128
bf16 = jnp.bfloat16
f32 = jnp.float32
MIB = 1024 * 1024


def from_y(a, d):
    return lax.ppermute(a, "gx", [(i, ((i // 2 - d) % 4) * 2 + i % 2) for i in range(8)])


def from_core(a):
    return lax.ppermute(a, "gx", [(i, i ^ 1) for i in range(8)])


def from_ring(a, d, leg):
    pairs = []
    for gx in range(8):
        for gy in range(16):
            z, x = gy // 4, gy % 4
            if gx % 2 == leg:
                x = (x - d) % 4
            else:
                z = (z - d) % 4
            pairs.append((gx * 16 + gy, gx * 16 + z * 4 + x))
    return lax.ppermute(a, ("gx", "gy"), pairs)


def total_of(parts):
    out = parts[0].astype(f32)
    for part in parts[1:]:
        out = out + part.astype(f32)
    return out


def attend_kernel(
    lengths_ref, got_ref, pair_ref, key_hbm, value_hbm, out_ref, key_ref, value_ref, sems
):
    copies = []
    for beam in range(4):
        copies.append(pltpu.make_async_copy(key_hbm.at[beam], key_ref.at[beam], sems.at[0, beam]))
        copies.append(
            pltpu.make_async_copy(value_hbm.at[beam], value_ref.at[beam], sems.at[1, beam])
        )
    for copy in copies:
        copy.start()
    group = (lax.broadcasted_iota(jnp.int32, (64, 1), 0) % 16) // 4
    score_scale = 1.0 / HD**0.5
    for copy in copies:
        copy.wait()
    for beam in range(4):
        got = got_ref[beam]
        query = jnp.concatenate([got[:, i * 128 : i * 128 + 128] for i in range(4)], 0)
        zero = jnp.zeros_like(query)
        wide = jnp.concatenate([jnp.where(group == g, query, zero) for g in range(4)], 1)
        pair = pair_ref[beam : beam + 1].astype(f32)
        scores = lax.dot_general(
            wide, key_ref[beam], (((1,), (1,)), ((), ())), preferred_element_type=f32
        )
        live = lax.broadcasted_iota(jnp.int32, scores.shape, 1) < lengths_ref[beam]
        scores = jnp.where(live, scores * score_scale, -jnp.inf)
        self_score = jnp.sum(wide.astype(f32) * pair[:, :512], axis=1, keepdims=True) * score_scale
        peak = jnp.maximum(jnp.max(scores, axis=1, keepdims=True), self_score)
        raw_weights = jnp.exp(scores - peak)
        self_weight = jnp.exp(self_score - peak)
        total = jnp.sum(raw_weights, axis=1, keepdims=True) + self_weight
        probs = (raw_weights / total).astype(bf16)
        own_prob = (self_weight / total).astype(bf16).astype(f32)
        mixed = jnp.dot(probs, value_ref[beam], preferred_element_type=f32)
        mixed = mixed + own_prob * pair[:, 512:]
        out = jnp.zeros((64, 128), f32)
        for g in range(4):
            out = out + jnp.where(group == g, mixed[:, g * 128 : g * 128 + 128], 0.0)
        out = out.astype(bf16)
        for i in range(4):
            out_ref[beam, :, i * 128 : i * 128 + 128] = out[i * 16 : i * 16 + 16]


def in_vmem(count):
    return [pl.BlockSpec(memory_space=pltpu.VMEM)] * count


def attend(got, pair, key_cache, value_cache, lengths):
    return pl.pallas_call(
        attend_kernel,
        out_shape=jax.ShapeDtypeStruct((4, 16, 512), bf16),
        in_specs=[pl.BlockSpec(memory_space=pltpu.SMEM)]
        + in_vmem(2)
        + [pl.BlockSpec(memory_space=pltpu.HBM)] * 2,
        out_specs=in_vmem(1)[0],
        scratch_shapes=[
            pltpu.VMEM((4, 256, 512), bf16),
            pltpu.VMEM((4, 256, 512), bf16),
            pltpu.SemaphoreType.DMA((2, 4)),
        ],
        compiler_params=pltpu.CompilerParams(vmem_limit_bytes=8 * MIB),
        cost_estimate=pl.CostEstimate(flops=10**8, bytes_accessed=2**21, transcendentals=65536),
    )(lengths, got, pair, key_cache, value_cache)


def stack_kernel(*refs):
    row = 0
    for ref in refs[:-1]:
        refs[-1][row : row + ref.shape[0]] = ref[...]
        row += ref.shape[0]


def stack(parts):
    rows, width = sum(part.shape[0] for part in parts), parts[0].shape[1]
    return pl.pallas_call(
        stack_kernel,
        out_shape=jax.ShapeDtypeStruct((rows, width), bf16),
        in_specs=in_vmem(len(parts)),
        out_specs=in_vmem(1)[0],
        compiler_params=pltpu.CompilerParams(vmem_limit_bytes=8 * MIB),
        cost_estimate=pl.CostEstimate(
            flops=0, bytes_accessed=4 * rows * width, transcendentals=0
        ),
    )(*parts)


def chunks_kernel(ids_ref, terms_ref, *out_refs):
    for k, out_ref in enumerate(out_refs):
        for j in range(4):
            at = pl.ds(pl.multiple_of(ids_ref[4 * k + j] * 128, 128), 128)
            out_ref[:, j * 128 : j * 128 + 128] = terms_ref[:, at]


def take_chunks(terms, ids):
    out = jax.ShapeDtypeStruct((terms.shape[0], 512), bf16)
    return pl.pallas_call(
        chunks_kernel,
        out_shape=(out,) * 4,
        in_specs=[pl.BlockSpec(memory_space=pltpu.SMEM)] + in_vmem(1),
        out_specs=tuple(in_vmem(4)),
        compiler_params=pltpu.CompilerParams(vmem_limit_bytes=8 * MIB),
        cost_estimate=pl.CostEstimate(flops=0, bytes_accessed=2**22, transcendentals=0),
    )(ids, terms)


def scatter_gy(terms, ids):
    chunks = take_chunks(terms, ids)
    moved = [chunks[0]] + [from_ring(chunks[k], (4 - k) % 4, 0) for k in (1, 3, 2)]

    def column_sum(j):
        return total_of([part[:, j * 128 : j * 128 + 128] for part in moved])

    last = [from_ring(column_sum(j).astype(bf16), (4 - j) % 4, 1) for j in (1, 3, 2)]
    return total_of([column_sum(0)] + last)


def gather_gy(rows):
    first = [from_ring(rows, k, 0) for k in (1, 3, 2)]
    first = stack([rows, first[0], first[2], first[1]])
    last = [from_ring(first, k, 1) for k in (1, 3, 2)]
    return [first, last[0], last[2], last[1]]


def scale_kernel(ids_ref, s0_ref, s1_ref, s2_ref, s3_ref, gain_ref, out_ref, square_ref):
    squares = jnp.zeros((512, 128), f32)
    for k, stack_ref in enumerate((s0_ref, s1_ref, s2_ref, s3_ref)):
        for j in range(4):
            chunk = ids_ref[4 * j + k]
            wide = stack_ref[j * 512 : j * 512 + 512].astype(f32)
            squares = squares + wide * wide
            scaled = (wide * gain_ref[pl.ds(chunk, 1), :]).astype(bf16)
            out_ref[:, pl.ds(pl.multiple_of(chunk * 128, 128), 128)] = scaled
    square = jnp.sum(squares, axis=1, keepdims=True)
    high = square.astype(bf16).astype(f32)
    low = (square - high).astype(bf16).astype(f32)
    lane = lax.broadcasted_iota(jnp.int32, (512, 128), 1)
    square_ref[...] = jnp.where(lane == 0, high, jnp.where(lane == 1, low, 0.0)).astype(bf16)


def scale_features(stacks, gain, ids):
    return pl.pallas_call(
        scale_kernel,
        out_shape=(
            jax.ShapeDtypeStruct((512, 2048), bf16),
            jax.ShapeDtypeStruct((512, 128), bf16),
        ),
        in_specs=[pl.BlockSpec(memory_space=pltpu.SMEM)] + in_vmem(5),
        out_specs=tuple(in_vmem(2)),
        compiler_params=pltpu.CompilerParams(vmem_limit_bytes=8 * MIB),
        cost_estimate=pl.CostEstimate(flops=2**33, bytes_accessed=2**25, transcendentals=0),
    )(ids, *stacks, gain)


def scatter_gx(other, same):
    moved = from_core(other)

    def row_sum(k):
        at = slice(64 * k, 64 * k + 64)
        return same[at].astype(f32) + moved[at].astype(f32)

    return [row_sum(0)] + [from_y(row_sum(k).astype(bf16), (4 - k) % 4) for k in (1, 3, 2)]


def gather_gx(rows):
    same = [rows] + [from_y(rows, k) for k in (1, 3, 2)]
    same = [same[0], same[1], same[3], same[2]]
    return stack(same + [from_core(part) for part in same])


def to_own_order(rows, y, core):
    blocks = rows.reshape(4, 2, 64, rows.shape[1])
    blocks = lax.dynamic_slice_in_dim(jnp.concatenate([blocks, blocks[:3]], 0), y, 4, 0)
    first, second = blocks[:, 0], blocks[:, 1]
    same = jnp.where(core == 0, first, second)
    other = jnp.where(core == 0, second, first)
    return jnp.concatenate([same, other], 0).reshape(rows.shape)


def from_own_order(rows, y, core):
    blocks = rows.reshape(2, 4, 64, rows.shape[1])
    blocks = lax.dynamic_slice_in_dim(
        jnp.concatenate([blocks, blocks[:, :3]], 1), (4 - y) & 3, 4, 1
    )
    first = jnp.where(core == 0, blocks[0], blocks[1])
    second = jnp.where(core == 0, blocks[1], blocks[0])
    return jnp.stack([first, second], 1).reshape(rows.shape)


def per_device(
    hidden,
    queries,
    new_kv,
    key_cache,
    value_cache,
    lengths,
    out_weight,
    norm_gain,
    w_gate,
    w_up,
    w_down,
):
    gx, gy = lax.axis_index("gx"), lax.axis_index("gy")
    y, core, z, x = gx >> 1, gx & 1, gy >> 2, gy & 3
    up_k, up_j = jnp.arange(16, dtype=jnp.int32) >> 2, jnp.arange(16, dtype=jnp.int32) & 3
    ids = jnp.where(
        core == 0,
        ((z + up_j) & 3) * 4 + ((x + up_k) & 3),
        ((z + up_k) & 3) * 4 + ((x + up_j) & 3),
    )
    gain_rows = jnp.broadcast_to(norm_gain.reshape(1, 4, 32), (16, 4, 32)).reshape(64, 32)
    sent = jnp.concatenate([queries, new_kv, gain_rows], 1)
    got = lax.all_to_all(sent.reshape(16, 4, 608), "gy", 0, 0, tiled=True)
    pair_rows = got[:, :, 512:576].transpose(1, 0, 2).reshape(4, 1024)
    gain = got[:, :, 576:].reshape(16, 128).astype(f32)
    attended = attend(got[:, :, :512].transpose(1, 0, 2), pair_rows, key_cache, value_cache, lengths)
    head_block = lax.all_to_all(attended, "gy", 1, 1, tiled=True)
    head_block = head_block.transpose(1, 0, 2).reshape(64, 512)
    heads = gather_gx(head_block)
    mine = to_own_order(hidden.T, y, core)
    terms = jnp.dot(heads, out_weight, preferred_element_type=f32).astype(bf16)
    resid = (mine.astype(f32) + scatter_gy(terms, ids)).astype(bf16)
    scaled, squares = scale_features(gather_gy(resid), gain, ids)
    gate = jnp.dot(scaled, w_gate, preferred_element_type=f32).astype(bf16)
    up = jnp.dot(scaled, w_up, preferred_element_type=f32).astype(bf16)
    gate_other = jnp.concatenate([gate[256:], squares[256:]], 1)
    gate_same = jnp.concatenate([gate[:256], squares[:256]], 1)
    gate_sum = total_of(scatter_gx(gate_other, gate_same))
    up_sum = total_of(scatter_gx(up[256:], up[:256]))
    square_sum = gate_sum[:, 1664:1665] + gate_sum[:, 1665:1666]
    scale = lax.rsqrt(square_sum / D + 1e-05)
    act = (jax.nn.silu(gate_sum[:, :1664] * scale) * (up_sum * scale)).astype(bf16)
    down_terms = jnp.dot(gather_gx(act), w_down, preferred_element_type=f32).astype(bf16)
    down = scatter_gy(down_terms, ids)
    mixed = (resid.astype(f32) + down).astype(bf16)
    return from_own_order(mixed, y, core).T


def solution(mesh):
    return jax.shard_map(
        per_device,
        mesh=mesh,
        in_specs=(
            P(("gx", "gy"), None),
            P("gx", "gy"),
            P("gx", "gy"),
            P(("gx", "gy"), None, None),
            P(("gx", "gy"), None, None),
            P(("gx", "gy")),
            P("gy", "gx"),
            P(("gx", "gy")),
            P("gx", "gy"),
            P("gx", "gy"),
            P("gy", "gx"),
        ),
        out_specs=P(("gx", "gy"), None),
        check_vma=False,
    )
```

```python
import jax
import jax.numpy as jnp
from jax import lax
from jax.experimental import pallas as pl
from jax.experimental.pallas import tpu as pltpu
from jax.sharding import PartitionSpec as P

D = 16384
HQ = 64
HK = 4
HD = 128
bf16 = jnp.bfloat16
f32 = jnp.float32
MIB = 1024 * 1024


def from_y(a, d):
    return lax.ppermute(a, "gx", [(i, ((i // 2 - d) % 4) * 2 + i % 2) for i in range(8)])


def from_core(a):
    return lax.ppermute(a, "gx", [(i, i ^ 1) for i in range(8)])


def from_ring(a, d, leg):
    pairs = []
    for gx in range(8):
        for gy in range(16):
            z, x = gy // 4, gy % 4
            if gx % 2 == leg:
                x = (x - d) % 4
            else:
                z = (z - d) % 4
            pairs.append((gx * 16 + gy, gx * 16 + z * 4 + x))
    return lax.ppermute(a, ("gx", "gy"), pairs)


def total_of(parts):
    out = parts[0].astype(f32)
    for part in parts[1:]:
        out = out + part.astype(f32)
    return out


def pack_kernel(query_ref, pair_ref, gain_ref, out_ref):
    query, pair = query_ref[...].astype(f32), pair_ref[...].astype(f32)
    gain = jnp.broadcast_to(gain_ref[...].astype(f32), (4, 128))
    for s in range(16):
        out_ref[s, :, :512] = query[4 * s : 4 * s + 4].astype(bf16)
        out_ref[s, :, 512:576] = pair[4 * s : 4 * s + 4].astype(bf16)
        out_ref[s, :, 640:] = gain.astype(bf16)


def pack(queries, new_kv, gain):
    return pl.pallas_call(
        pack_kernel,
        out_shape=jax.ShapeDtypeStruct((16, 4, 768), bf16),
        in_specs=in_vmem(3),
        out_specs=in_vmem(1)[0],
        compiler_params=pltpu.CompilerParams(vmem_limit_bytes=4 * MIB),
        cost_estimate=pl.CostEstimate(flops=2**33, bytes_accessed=2**24, transcendentals=0),
    )(queries, new_kv, gain.reshape(1, 128))


def attend_kernel(lengths_ref, got_ref, pair_ref, key_ref, value_ref, out_ref):
    group = (lax.broadcasted_iota(jnp.int32, (64, 1), 0) % 16) // 4
    score_scale = 1.0 / HD**0.5
    for beam in range(4):
        got = got_ref[beam]
        query = jnp.concatenate([got[:, i * 128 : i * 128 + 128] for i in range(4)], 0)
        zero = jnp.zeros_like(query)
        wide = jnp.concatenate([jnp.where(group == g, query, zero) for g in range(4)], 1)
        pair = pair_ref[beam : beam + 1].astype(f32)
        scores = lax.dot_general(
            wide, key_ref[beam], (((1,), (1,)), ((), ())), preferred_element_type=f32
        )
        live = lax.broadcasted_iota(jnp.int32, scores.shape, 1) < lengths_ref[beam]
        scores = jnp.where(live, scores * score_scale, -jnp.inf)
        self_score = jnp.sum(wide.astype(f32) * pair[:, :512], axis=1, keepdims=True) * score_scale
        peak = jnp.maximum(jnp.max(scores, axis=1, keepdims=True), self_score)
        raw_weights = jnp.exp(scores - peak)
        self_weight = jnp.exp(self_score - peak)
        total = jnp.sum(raw_weights, axis=1, keepdims=True) + self_weight
        probs = (raw_weights / total).astype(bf16)
        own_prob = (self_weight / total).astype(bf16).astype(f32)
        mixed = jnp.dot(probs, value_ref[beam], preferred_element_type=f32)
        mixed = mixed + own_prob * pair[:, 512:]
        out = jnp.zeros((64, 128), f32)
        for g in range(4):
            out = out + jnp.where(group == g, mixed[:, g * 128 : g * 128 + 128], 0.0)
        out = out.astype(bf16)
        for i in range(4):
            out_ref[beam, :, i * 128 : i * 128 + 128] = out[i * 16 : i * 16 + 16]


def in_vmem(count):
    return [pl.BlockSpec(memory_space=pltpu.VMEM)] * count


def attend(got, pair, key_cache, value_cache, lengths):
    return pl.pallas_call(
        attend_kernel,
        out_shape=jax.ShapeDtypeStruct((4, 16, 512), bf16),
        in_specs=[pl.BlockSpec(memory_space=pltpu.SMEM)] + in_vmem(4),
        out_specs=in_vmem(1)[0],
        compiler_params=pltpu.CompilerParams(vmem_limit_bytes=8 * MIB),
        cost_estimate=pl.CostEstimate(flops=10**8, bytes_accessed=2**21, transcendentals=65536),
    )(lengths, got, pair, key_cache, value_cache)


def stack_kernel(*refs):
    row = 0
    for ref in refs[:-1]:
        refs[-1][row : row + ref.shape[0]] = ref[...]
        row += ref.shape[0]


def stack(parts):
    rows, width = sum(part.shape[0] for part in parts), parts[0].shape[1]
    return pl.pallas_call(
        stack_kernel,
        out_shape=jax.ShapeDtypeStruct((rows, width), bf16),
        in_specs=in_vmem(len(parts)),
        out_specs=in_vmem(1)[0],
        compiler_params=pltpu.CompilerParams(vmem_limit_bytes=8 * MIB),
        cost_estimate=pl.CostEstimate(
            flops=0, bytes_accessed=4 * rows * width, transcendentals=0
        ),
    )(*parts)


def chunks_kernel(ids_ref, terms_ref, *out_refs):
    for k, out_ref in enumerate(out_refs):
        for j in range(4):
            at = pl.ds(pl.multiple_of(ids_ref[4 * k + j] * 128, 128), 128)
            out_ref[:, j * 128 : j * 128 + 128] = terms_ref[:, at]


def take_chunks(terms, ids):
    out = jax.ShapeDtypeStruct((terms.shape[0], 512), bf16)
    return pl.pallas_call(
        chunks_kernel,
        out_shape=(out,) * 4,
        in_specs=[pl.BlockSpec(memory_space=pltpu.SMEM)] + in_vmem(1),
        out_specs=tuple(in_vmem(4)),
        compiler_params=pltpu.CompilerParams(vmem_limit_bytes=8 * MIB),
        cost_estimate=pl.CostEstimate(flops=0, bytes_accessed=2**22, transcendentals=0),
    )(ids, terms)


def scatter_gy(terms, ids):
    chunks = take_chunks(terms, ids)
    moved = [chunks[0]] + [from_ring(chunks[k], (4 - k) % 4, 0) for k in (1, 3, 2)]

    def column_sum(j):
        return total_of([part[:, j * 128 : j * 128 + 128] for part in moved])

    last = [from_ring(column_sum(j).astype(bf16), (4 - j) % 4, 1) for j in (1, 3, 2)]
    return total_of([column_sum(0)] + last)


def gather_gy(rows):
    first = [from_ring(rows, k, 0) for k in (1, 3, 2)]
    first = stack([rows, first[0], first[2], first[1]])
    last = [from_ring(first, k, 1) for k in (1, 3, 2)]
    return [first, last[0], last[2], last[1]]


def scale_kernel(
    ids_ref, s0_ref, s1_ref, s2_ref, s3_ref, gain_ref, same_ref, other_ref, square_ref
):
    squares = jnp.zeros((512, 128), f32)
    for k, stack_ref in enumerate((s0_ref, s1_ref, s2_ref, s3_ref)):
        for j in range(4):
            chunk = ids_ref[4 * j + k]
            wide = stack_ref[j * 512 : j * 512 + 512].astype(f32)
            squares = squares + wide * wide
            scaled = (wide * gain_ref[pl.ds(chunk, 1), :]).astype(bf16)
            at = pl.ds(pl.multiple_of(chunk * 128, 128), 128)
            same_ref[:, at] = scaled[:256]
            other_ref[:, at] = scaled[256:]
    square = jnp.sum(squares, axis=1, keepdims=True)
    high = square.astype(bf16).astype(f32)
    low = (square - high).astype(bf16).astype(f32)
    lane = lax.broadcasted_iota(jnp.int32, (512, 128), 1)
    square_ref[...] = jnp.where(lane == 0, high, jnp.where(lane == 1, low, 0.0)).astype(bf16)


def scale_features(stacks, gain, ids):
    return pl.pallas_call(
        scale_kernel,
        out_shape=(
            jax.ShapeDtypeStruct((256, 2048), bf16),
            jax.ShapeDtypeStruct((256, 2048), bf16),
            jax.ShapeDtypeStruct((512, 128), bf16),
        ),
        in_specs=[pl.BlockSpec(memory_space=pltpu.SMEM)] + in_vmem(5),
        out_specs=tuple(in_vmem(3)),
        compiler_params=pltpu.CompilerParams(vmem_limit_bytes=8 * MIB),
        cost_estimate=pl.CostEstimate(flops=2**33, bytes_accessed=2**25, transcendentals=0),
    )(ids, *stacks, gain)


def pair_kernel(gate_ref, up_ref, square_ref, moved_gate_ref, moved_up_ref, *out_refs):
    for k, out_ref in enumerate(out_refs):
        at = slice(64 * k, 64 * k + 64)
        gate = gate_ref[at, :].astype(f32) + moved_gate_ref[at, :].astype(f32)
        up = up_ref[at, :].astype(f32) + moved_up_ref[at, :1664].astype(f32)
        square = square_ref[at, :].astype(f32) + moved_up_ref[at, 1664:].astype(f32)
        if k:
            square = jnp.sum(square, axis=1, keepdims=True)
            high = square.astype(bf16).astype(f32)
            lane = lax.broadcasted_iota(jnp.int32, (64, 128), 1)
            square = jnp.where(lane == 0, high, jnp.where(lane == 1, square - high, 0.0))
        out_ref[:, :1664] = gate.astype(out_ref.dtype)
        out_ref[:, 1664:3328] = up.astype(out_ref.dtype)
        out_ref[:, 3328:] = square.astype(out_ref.dtype)


def act_kernel(own_ref, a_ref, b_ref, c_ref, out_ref):
    def total(at):
        moved = [ref[:, at].astype(f32) for ref in (a_ref, b_ref, c_ref)]
        return own_ref[:, at] + moved[0] + moved[1] + moved[2]

    square = jnp.sum(total(slice(3328, 3456)), axis=1, keepdims=True)
    scale = lax.rsqrt(square / D + 1e-05)
    gate, up = total(slice(0, 1664)) * scale, total(slice(1664, 3328)) * scale
    out_ref[...] = (gate / (1.0 + jnp.exp(-gate)) * up).astype(bf16)


def local(kernel, out_shape, *args):
    many = isinstance(out_shape, tuple)
    return pl.pallas_call(
        kernel,
        out_shape=out_shape,
        in_specs=in_vmem(len(args)),
        out_specs=tuple(in_vmem(len(out_shape))) if many else in_vmem(1)[0],
        compiler_params=pltpu.CompilerParams(vmem_limit_bytes=12 * MIB),
        cost_estimate=pl.CostEstimate(flops=2**22, bytes_accessed=2**22, transcendentals=0),
    )(*args)


def gather_gx(rows):
    same = [rows] + [from_y(rows, k) for k in (1, 3, 2)]
    same = stack([same[0], same[1], same[3], same[2]])
    return stack([same, from_core(same)])


def to_own_order(rows, y, core):
    blocks = rows.reshape(4, 2, 64, rows.shape[1])
    blocks = lax.dynamic_slice_in_dim(jnp.concatenate([blocks, blocks[:3]], 0), y, 4, 0)
    first, second = blocks[:, 0], blocks[:, 1]
    same = jnp.where(core == 0, first, second)
    other = jnp.where(core == 0, second, first)
    return jnp.concatenate([same, other], 0).reshape(rows.shape)


def from_own_order(rows, y, core):
    blocks = rows.reshape(2, 4, 64, rows.shape[1])
    blocks = lax.dynamic_slice_in_dim(
        jnp.concatenate([blocks, blocks[:, :3]], 1), (4 - y) & 3, 4, 1
    )
    first = jnp.where(core == 0, blocks[0], blocks[1])
    second = jnp.where(core == 0, blocks[1], blocks[0])
    return jnp.stack([first, second], 1).reshape(rows.shape)


def per_device(
    hidden,
    queries,
    new_kv,
    key_cache,
    value_cache,
    lengths,
    out_weight,
    norm_gain,
    w_gate,
    w_up,
    w_down,
):
    gx, gy = lax.axis_index("gx"), lax.axis_index("gy")
    y, core, z, x = gx >> 1, gx & 1, gy >> 2, gy & 3
    up_k, up_j = jnp.arange(16, dtype=jnp.int32) >> 2, jnp.arange(16, dtype=jnp.int32) & 3
    ids = jnp.where(
        core == 0,
        ((z + up_j) & 3) * 4 + ((x + up_k) & 3),
        ((z + up_k) & 3) * 4 + ((x + up_j) & 3),
    )
    got = lax.all_to_all(pack(queries, new_kv, norm_gain), "gy", 0, 0, tiled=True)
    pair_rows = got[:, :, 512:576].transpose(1, 0, 2).reshape(4, 1024)
    gain = got[:, 0, 640:].astype(f32)
    attended = attend(got[:, :, :512].transpose(1, 0, 2), pair_rows, key_cache, value_cache, lengths)
    head_block = lax.all_to_all(attended, "gy", 1, 1, tiled=True)
    head_block = head_block.transpose(1, 0, 2).reshape(64, 512)
    heads = gather_gx(head_block)
    mine = to_own_order(hidden.T, y, core)
    terms = jnp.dot(heads, out_weight, preferred_element_type=f32).astype(bf16)
    resid = (mine.astype(f32) + scatter_gy(terms, ids)).astype(bf16)
    same, other, squares = scale_features(gather_gy(resid), gain, ids)

    def product(a, b):
        return jnp.dot(a, b, preferred_element_type=f32).astype(bf16)

    gate_moved = from_core(product(other, w_gate))
    up_moved = from_core(jnp.concatenate([product(other, w_up), squares[256:]], 1))
    message = jax.ShapeDtypeStruct((64, 3456), bf16)
    own = jax.ShapeDtypeStruct((64, 3456), f32)
    pairs = local(
        pair_kernel,
        (own, message, message, message),
        product(same, w_gate),
        product(same, w_up),
        squares[:256],
        gate_moved,
        up_moved,
    )
    moved = [from_y(pairs[k], (4 - k) % 4) for k in (1, 3, 2)]
    act = local(act_kernel, jax.ShapeDtypeStruct((64, 1664), bf16), pairs[0], *moved)
    down_terms = jnp.dot(gather_gx(act), w_down, preferred_element_type=f32).astype(bf16)
    down = scatter_gy(down_terms, ids)
    mixed = (resid.astype(f32) + down).astype(bf16)
    return from_own_order(mixed, y, core).T


def solution(mesh):
    return jax.shard_map(
        per_device,
        mesh=mesh,
        in_specs=(
            P(("gx", "gy"), None),
            P("gx", "gy"),
            P("gx", "gy"),
            P(("gx", "gy"), None, None),
            P(("gx", "gy"), None, None),
            P(("gx", "gy")),
            P("gy", "gx"),
            P(("gx", "gy")),
            P("gx", "gy"),
            P("gx", "gy"),
            P("gy", "gx"),
        ),
        out_specs=P(("gx", "gy"), None),
        check_vma=False,
    )
```

```python
import jax
import jax.numpy as jnp
from jax import lax
from jax.experimental import pallas as pl
from jax.experimental.pallas import tpu as pltpu
from jax.sharding import PartitionSpec as P

D = 16384
HQ = 64
HK = 4
HD = 128
bf16 = jnp.bfloat16
f32 = jnp.float32
MIB = 1024 * 1024


def from_y(a, d):
    return lax.ppermute(a, "gx", [(i, ((i // 2 - d) % 4) * 2 + i % 2) for i in range(8)])


def from_core(a):
    return lax.ppermute(a, "gx", [(i, i ^ 1) for i in range(8)])


def from_ring(a, d, leg):
    pairs = []
    for gx in range(8):
        for gy in range(16):
            z, x = gy // 4, gy % 4
            if gx % 2 == leg:
                x = (x - d) % 4
            else:
                z = (z - d) % 4
            pairs.append((gx * 16 + gy, gx * 16 + z * 4 + x))
    return lax.ppermute(a, ("gx", "gy"), pairs)


def total_of(parts):
    out = parts[0].astype(f32)
    for part in parts[1:]:
        out = out + part.astype(f32)
    return out


def pack_kernel(query_ref, pair_ref, gain_ref, out_ref):
    query, pair = query_ref[...].astype(f32), pair_ref[...].astype(f32)
    gain = jnp.broadcast_to(gain_ref[...].astype(f32), (4, 128))
    for s in range(16):
        out_ref[s, :, :512] = query[4 * s : 4 * s + 4].astype(bf16)
        out_ref[s, :, 512:576] = pair[4 * s : 4 * s + 4].astype(bf16)
        out_ref[s, :, 640:] = gain.astype(bf16)


def pack(queries, new_kv, gain):
    return pl.pallas_call(
        pack_kernel,
        out_shape=jax.ShapeDtypeStruct((16, 4, 768), bf16),
        compiler_params=pltpu.CompilerParams(vmem_limit_bytes=4 * MIB),
        cost_estimate=pl.CostEstimate(flops=2**35, bytes_accessed=2**24, transcendentals=0),
    )(queries, new_kv, gain.reshape(1, 128))


def attend_kernel(lengths_ref, got_ref, pair_ref, key_ref, value_ref, out_ref):
    group = (lax.broadcasted_iota(jnp.int32, (64, 1), 0) % 16) // 4
    score_scale = 1.0 / HD**0.5
    for beam in range(4):
        got = got_ref[beam]
        query = jnp.concatenate([got[:, i * 128 : i * 128 + 128] for i in range(4)], 0)
        zero = jnp.zeros_like(query)
        wide = jnp.concatenate([jnp.where(group == g, query, zero) for g in range(4)], 1)
        pair = pair_ref[beam : beam + 1].astype(f32)
        scores = lax.dot_general(
            wide, key_ref[beam], (((1,), (1,)), ((), ())), preferred_element_type=f32
        )
        live = lax.broadcasted_iota(jnp.int32, scores.shape, 1) < lengths_ref[beam]
        scores = jnp.where(live, scores * score_scale, -jnp.inf)
        self_score = jnp.sum(wide.astype(f32) * pair[:, :512], axis=1, keepdims=True) * score_scale
        peak = jnp.maximum(jnp.max(scores, axis=1, keepdims=True), self_score)
        raw_weights = jnp.exp(scores - peak)
        self_weight = jnp.exp(self_score - peak)
        total = jnp.sum(raw_weights, axis=1, keepdims=True) + self_weight
        probs = (raw_weights / total).astype(bf16)
        own_prob = (self_weight / total).astype(bf16).astype(f32)
        mixed = jnp.dot(probs, value_ref[beam], preferred_element_type=f32)
        mixed = mixed + own_prob * pair[:, 512:]
        out = jnp.zeros((64, 128), f32)
        for g in range(4):
            out = out + jnp.where(group == g, mixed[:, g * 128 : g * 128 + 128], 0.0)
        out = out.astype(bf16)
        for i in range(4):
            out_ref[beam, :, i * 128 : i * 128 + 128] = out[i * 16 : i * 16 + 16]


def in_vmem(count):
    return [pl.BlockSpec(memory_space=pltpu.VMEM)] * count


def attend(got, pair, key_cache, value_cache, lengths):
    return pl.pallas_call(
        attend_kernel,
        out_shape=jax.ShapeDtypeStruct((4, 16, 512), bf16),
        in_specs=[pl.BlockSpec(memory_space=pltpu.SMEM)] + in_vmem(4),
        out_specs=in_vmem(1)[0],
        compiler_params=pltpu.CompilerParams(vmem_limit_bytes=8 * MIB),
        cost_estimate=pl.CostEstimate(flops=10**8, bytes_accessed=2**21, transcendentals=65536),
    )(lengths, got, pair, key_cache, value_cache)


def stack_kernel(*refs):
    row = 0
    for ref in refs[:-1]:
        refs[-1][row : row + ref.shape[0]] = ref[...]
        row += ref.shape[0]


def stack(parts):
    rows, width = sum(part.shape[0] for part in parts), parts[0].shape[1]
    return pl.pallas_call(
        stack_kernel,
        out_shape=jax.ShapeDtypeStruct((rows, width), bf16),
        in_specs=in_vmem(len(parts)),
        out_specs=in_vmem(1)[0],
        compiler_params=pltpu.CompilerParams(vmem_limit_bytes=8 * MIB),
        cost_estimate=pl.CostEstimate(
            flops=0, bytes_accessed=4 * rows * width, transcendentals=0
        ),
    )(*parts)


def chunks_kernel(ids_ref, same_ref, other_ref, *out_refs):
    for k, out_ref in enumerate(out_refs):
        for j in range(4):
            at = pl.ds(pl.multiple_of(ids_ref[4 * k + j] * 128, 128), 128)
            out_ref[:256, j * 128 : j * 128 + 128] = same_ref[:, at]
            out_ref[256:, j * 128 : j * 128 + 128] = other_ref[:, at]


def product(a, b):
    return jnp.dot(a, b, preferred_element_type=f32).astype(bf16)


def take_chunks(terms, ids):
    out = jax.ShapeDtypeStruct((512, 512), bf16)
    return pl.pallas_call(
        chunks_kernel,
        out_shape=(out,) * 4,
        in_specs=[pl.BlockSpec(memory_space=pltpu.SMEM)] + in_vmem(2),
        out_specs=tuple(in_vmem(4)),
        compiler_params=pltpu.CompilerParams(vmem_limit_bytes=8 * MIB),
        cost_estimate=pl.CostEstimate(flops=0, bytes_accessed=2**22, transcendentals=0),
    )(ids, *terms)


def sum_kernel(a_ref, b_ref, c_ref, d_ref, *out_refs):
    for j, out_ref in enumerate(out_refs):
        at = slice(j * 128, j * 128 + 128)
        out_ref[...] = total_of([ref[:, at] for ref in (a_ref, b_ref, c_ref, d_ref)]).astype(
            out_ref.dtype
        )


def scatter_gy(terms, ids):
    chunks = take_chunks(terms, ids)
    moved = [chunks[0]] + [from_ring(chunks[k], (4 - k) % 4, 0) for k in (1, 3, 2)]

    part, own = (jax.ShapeDtypeStruct((512, 128), dtype) for dtype in (bf16, f32))
    sums = local(sum_kernel, (own, part, part, part), *moved)
    return [sums[0]] + [from_ring(sums[j], (4 - j) % 4, 1) for j in (1, 3, 2)]


def gather_gy(rows):
    first = [from_ring(rows, k, 0) for k in (1, 3, 2)]
    first = stack([rows, first[0], first[2], first[1]])
    last = [from_ring(first, k, 1) for k in (1, 3, 2)]
    return [first, last[0], last[2], last[1]]


def scale_kernel(
    ids_ref, s0_ref, s1_ref, s2_ref, s3_ref, gain_ref, same_ref, other_ref, square_ref
):
    squares = jnp.zeros((512, 128), f32)
    for k, stack_ref in enumerate((s0_ref, s1_ref, s2_ref, s3_ref)):
        for j in range(4):
            chunk = ids_ref[4 * j + k]
            wide = stack_ref[j * 512 : j * 512 + 512].astype(f32)
            squares = squares + wide * wide
            scaled = (wide * gain_ref[pl.ds(chunk, 1), :]).astype(bf16)
            at = pl.ds(pl.multiple_of(chunk * 128, 128), 128)
            same_ref[:, at] = scaled[:256]
            other_ref[:, at] = scaled[256:]
    square = jnp.sum(squares, axis=1, keepdims=True)
    high = square.astype(bf16).astype(f32)
    low = (square - high).astype(bf16).astype(f32)
    lane = lax.broadcasted_iota(jnp.int32, (512, 128), 1)
    square_ref[...] = jnp.where(lane == 0, high, jnp.where(lane == 1, low, 0.0)).astype(bf16)


def scale_features(stacks, gain, ids):
    return pl.pallas_call(
        scale_kernel,
        out_shape=(
            jax.ShapeDtypeStruct((256, 2048), bf16),
            jax.ShapeDtypeStruct((256, 2048), bf16),
            jax.ShapeDtypeStruct((512, 128), bf16),
        ),
        in_specs=[pl.BlockSpec(memory_space=pltpu.SMEM)] + in_vmem(5),
        out_specs=tuple(in_vmem(3)),
        compiler_params=pltpu.CompilerParams(vmem_limit_bytes=8 * MIB),
        cost_estimate=pl.CostEstimate(flops=2**33, bytes_accessed=2**25, transcendentals=0),
    )(ids, *stacks, gain)


def high_and_low(square):
    square = jnp.sum(square, axis=1, keepdims=True)
    high = square.astype(bf16).astype(f32)
    lane = lax.broadcasted_iota(jnp.int32, (square.shape[0], 128), 1)
    return jnp.where(lane == 0, high, jnp.where(lane == 1, square - high, 0.0))


def pair_kernel(gate_ref, up_ref, square_ref, moved_gate_ref, moved_up_ref, *out_refs):
    row = 0
    for out_ref in out_refs:
        at = slice(row, row + out_ref.shape[0])
        row += out_ref.shape[0]
        gate = gate_ref[at, :].astype(f32) + moved_gate_ref[at, :].astype(f32)
        up = up_ref[at, :].astype(f32) + moved_up_ref[at, :1664].astype(f32)
        square = square_ref[at, :].astype(f32) + moved_up_ref[at, 1664:].astype(f32)
        out_ref[:, :1664] = gate.astype(out_ref.dtype)
        out_ref[:, 1664:3328] = up.astype(out_ref.dtype)
        out_ref[:, 3328:] = high_and_low(square).astype(out_ref.dtype)


def relay_kernel(mine_ref, moved_ref, out_ref):
    out_ref[:, :3328] = (
        mine_ref[:, :3328].astype(f32) + moved_ref[:, :3328].astype(f32)
    ).astype(bf16)
    square = mine_ref[:, 3328:].astype(f32) + moved_ref[:, 3328:].astype(f32)
    out_ref[:, 3328:] = high_and_low(square).astype(bf16)


def act_kernel(own_ref, a_ref, b_ref, c_ref, d_ref, out_ref):
    for rows, refs in ((slice(0, 32), (a_ref, c_ref)), (slice(32, 64), (b_ref, d_ref))):

        def total(at):
            return own_ref[rows, at] + refs[0][:, at].astype(f32) + refs[1][:, at].astype(f32)

        square = jnp.sum(total(slice(3328, 3456)), axis=1, keepdims=True)
        scale = lax.rsqrt(square / D + 1e-05)
        gate, up = total(slice(0, 1664)) * scale, total(slice(1664, 3328)) * scale
        out_ref[rows, :] = (gate / (1.0 + jnp.exp(-gate)) * up).astype(bf16)


def relay(move, add, halves):
    (first_a, first_b), (second_a, second_b), (third_a, third_b) = halves
    moved_a, moved_b = move(second_a, 3), move(second_b, 1)
    below_b, above_a = move(first_b, 3), move(third_a, 1)
    below_a, above_b = move(add(first_a, moved_a), 3), move(add(third_b, moved_b), 1)
    return below_a, below_b, above_a, above_b


def local(kernel, out_shape, *args):
    many = isinstance(out_shape, tuple)
    return pl.pallas_call(
        kernel,
        out_shape=out_shape,
        in_specs=in_vmem(len(args)),
        out_specs=tuple(in_vmem(len(out_shape))) if many else in_vmem(1)[0],
        compiler_params=pltpu.CompilerParams(vmem_limit_bytes=12 * MIB),
        cost_estimate=pl.CostEstimate(flops=2**22, bytes_accessed=2**22, transcendentals=0),
    )(*args)


def gather_gx(rows):
    same = [rows] + [from_y(rows, k) for k in (1, 3, 2)]
    same = stack([same[0], same[1], same[3], same[2]])
    return same, from_core(same)


def own_order_kernel(blocks_ref, hidden_ref, out_ref, turned_ref):
    turned_ref[...] = hidden_ref[...].astype(f32).T
    for m in range(8):
        at = pl.ds(pl.multiple_of(blocks_ref[m] * 64, 64), 64)
        out_ref[64 * m : 64 * m + 64] = turned_ref[at, :].astype(bf16)


def final_kernel(blocks_ref, resid_ref, a_ref, b_ref, c_ref, d_ref, out_ref, total_ref):
    total = total_of([ref[...] for ref in (resid_ref, a_ref, b_ref, c_ref, d_ref)])
    for m in range(8):
        at = pl.ds(pl.multiple_of(blocks_ref[m] * 64, 64), 64)
        total_ref[at, :] = total[64 * m : 64 * m + 64]
    out_ref[...] = total_ref[...].T.astype(bf16)


def reorder(kernel, shape, blocks, *args):
    return pl.pallas_call(
        kernel,
        out_shape=jax.ShapeDtypeStruct(shape, bf16),
        in_specs=[pl.BlockSpec(memory_space=pltpu.SMEM)] + in_vmem(len(args)),
        out_specs=in_vmem(1)[0],
        scratch_shapes=[pltpu.VMEM((512, 128), f32)],
        compiler_params=pltpu.CompilerParams(vmem_limit_bytes=4 * MIB),
        cost_estimate=pl.CostEstimate(flops=2**20, bytes_accessed=2**20, transcendentals=0),
    )(blocks, *args)


def per_device(
    hidden,
    queries,
    new_kv,
    key_cache,
    value_cache,
    lengths,
    out_weight,
    norm_gain,
    w_gate,
    w_up,
    w_down,
):
    gx, gy = lax.axis_index("gx"), lax.axis_index("gy")
    y, core, z, x = gx >> 1, gx & 1, gy >> 2, gy & 3
    up_k, up_j = jnp.arange(16, dtype=jnp.int32) >> 2, jnp.arange(16, dtype=jnp.int32) & 3
    ids = jnp.where(
        core == 0,
        ((z + up_j) & 3) * 4 + ((x + up_k) & 3),
        ((z + up_k) & 3) * 4 + ((x + up_j) & 3),
    )
    got = lax.all_to_all(pack(queries, new_kv, norm_gain), "gy", 0, 0, tiled=True)
    pair_rows = got[:, :, 512:576].transpose(1, 0, 2).reshape(4, 1024)
    gain = got[:, 0, 640:].astype(f32)
    attended = attend(got[:, :, :512].transpose(1, 0, 2), pair_rows, key_cache, value_cache, lengths)
    head_block = lax.all_to_all(attended, "gy", 1, 1, tiled=True)
    head_block = head_block.transpose(1, 0, 2).reshape(64, 512)
    heads = gather_gx(head_block)
    block = jnp.arange(8, dtype=jnp.int32)
    blocks = ((y + (block & 3)) & 3) * 2 + (core ^ (block >> 2))
    mine = reorder(own_order_kernel, (512, 128), blocks, hidden)
    terms = [product(half, out_weight) for half in heads]
    resid = total_of([mine] + scatter_gy(terms, ids)).astype(bf16)
    same, other, squares = scale_features(gather_gy(resid), gain, ids)

    gate_moved = from_core(product(other, w_gate))
    up_moved = from_core(jnp.concatenate([product(other, w_up), squares[256:]], 1))
    message = jax.ShapeDtypeStruct((32, 3456), bf16)
    own, *pairs = local(
        pair_kernel,
        (jax.ShapeDtypeStruct((64, 3456), f32),) + (message,) * 6,
        product(same, w_gate),
        product(same, w_up),
        squares[:256],
        gate_moved,
        up_moved,
    )
    moved = relay(
        from_y,
        lambda mine, other: local(relay_kernel, message, mine, other),
        (pairs[:2], pairs[2:4], pairs[4:]),
    )
    act = local(act_kernel, jax.ShapeDtypeStruct((64, 1664), bf16), own, *moved)
    terms = [product(half, w_down) for half in gather_gx(act)]
    return reorder(final_kernel, (128, 512), blocks, resid, *scatter_gy(terms, ids))


def solution(mesh):
    return jax.shard_map(
        per_device,
        mesh=mesh,
        in_specs=(
            P(("gx", "gy"), None),
            P("gx", "gy"),
            P("gx", "gy"),
            P(("gx", "gy"), None, None),
            P(("gx", "gy"), None, None),
            P(("gx", "gy")),
            P("gy", "gx"),
            P(("gx", "gy")),
            P("gx", "gy"),
            P("gx", "gy"),
            P("gy", "gx"),
        ),
        out_specs=P(("gx", "gy"), None),
        check_vma=False,
    )
```

```python
import jax
import jax.numpy as jnp
from jax import lax
from jax.experimental import pallas as pl
from jax.experimental.pallas import tpu as pltpu
from jax.sharding import PartitionSpec as P

D = 16384
HQ = 64
HK = 4
HD = 128
bf16 = jnp.bfloat16
f32 = jnp.float32
MIB = 1024 * 1024


def from_y(a, d):
    return lax.ppermute(a, "gx", [(i, ((i // 2 - d) % 4) * 2 + i % 2) for i in range(8)])


def from_core(a):
    return lax.ppermute(a, "gx", [(i, i ^ 1) for i in range(8)])


def from_ring(a, d, leg):
    pairs = []
    for gx in range(8):
        for gy in range(16):
            z, x = gy // 4, gy % 4
            if gx % 2 == leg:
                x = (x - d) % 4
            else:
                z = (z - d) % 4
            pairs.append((gx * 16 + gy, gx * 16 + z * 4 + x))
    return lax.ppermute(a, ("gx", "gy"), pairs)


def total_of(parts):
    out = parts[0].astype(f32)
    for part in parts[1:]:
        out = out + part.astype(f32)
    return out


def pack_kernel(query_ref, pair_ref, gain_ref, out_ref):
    query, pair = query_ref[...].astype(f32), pair_ref[...].astype(f32)
    gain = jnp.broadcast_to(gain_ref[...].astype(f32), (4, 128))
    for s in range(16):
        out_ref[s, :, :512] = query[4 * s : 4 * s + 4].astype(bf16)
        out_ref[s, :, 512:576] = pair[4 * s : 4 * s + 4].astype(bf16)
        out_ref[s, :, 640:] = gain.astype(bf16)


def pack(queries, new_kv, gain):
    return pl.pallas_call(
        pack_kernel,
        out_shape=jax.ShapeDtypeStruct((16, 4, 768), bf16),
        compiler_params=pltpu.CompilerParams(vmem_limit_bytes=4 * MIB),
        cost_estimate=pl.CostEstimate(flops=2**35, bytes_accessed=2**24, transcendentals=0),
    )(queries, new_kv, gain.reshape(1, 128))


def attend_kernel(lengths_ref, got_ref, pair_ref, key_ref, value_ref, out_ref):
    group = (lax.broadcasted_iota(jnp.int32, (64, 1), 0) % 16) // 4
    score_scale = 1.0 / HD**0.5
    for beam in range(4):
        got = got_ref[beam]
        query = jnp.concatenate([got[:, i * 128 : i * 128 + 128] for i in range(4)], 0)
        zero = jnp.zeros_like(query)
        wide = jnp.concatenate([jnp.where(group == g, query, zero) for g in range(4)], 1)
        pair = pair_ref[beam : beam + 1].astype(f32)
        scores = lax.dot_general(
            wide, key_ref[beam], (((1,), (1,)), ((), ())), preferred_element_type=f32
        )
        live = lax.broadcasted_iota(jnp.int32, scores.shape, 1) < lengths_ref[beam]
        scores = jnp.where(live, scores * score_scale, -jnp.inf)
        self_score = jnp.sum(wide.astype(f32) * pair[:, :512], axis=1, keepdims=True) * score_scale
        peak = jnp.maximum(jnp.max(scores, axis=1, keepdims=True), self_score)
        raw_weights = jnp.exp(scores - peak)
        self_weight = jnp.exp(self_score - peak)
        total = jnp.sum(raw_weights, axis=1, keepdims=True) + self_weight
        probs = (raw_weights / total).astype(bf16)
        own_prob = (self_weight / total).astype(bf16).astype(f32)
        mixed = jnp.dot(probs, value_ref[beam], preferred_element_type=f32)
        mixed = mixed + own_prob * pair[:, 512:]
        out = jnp.zeros((64, 128), f32)
        for g in range(4):
            out = out + jnp.where(group == g, mixed[:, g * 128 : g * 128 + 128], 0.0)
        out = out.astype(bf16)
        for i in range(4):
            out_ref[beam, :, i * 128 : i * 128 + 128] = out[i * 16 : i * 16 + 16]


def in_vmem(count):
    return [pl.BlockSpec(memory_space=pltpu.VMEM)] * count


def attend(got, pair, key_cache, value_cache, lengths):
    return pl.pallas_call(
        attend_kernel,
        out_shape=jax.ShapeDtypeStruct((4, 16, 512), bf16),
        in_specs=[pl.BlockSpec(memory_space=pltpu.SMEM)] + in_vmem(4),
        out_specs=in_vmem(1)[0],
        compiler_params=pltpu.CompilerParams(vmem_limit_bytes=8 * MIB),
        cost_estimate=pl.CostEstimate(flops=10**8, bytes_accessed=2**21, transcendentals=65536),
    )(lengths, got, pair, key_cache, value_cache)


def stack_kernel(*refs):
    row = 0
    for ref in refs[:-1]:
        refs[-1][row : row + ref.shape[0]] = ref[...]
        row += ref.shape[0]


def stack(parts):
    rows, width = sum(part.shape[0] for part in parts), parts[0].shape[1]
    return pl.pallas_call(
        stack_kernel,
        out_shape=jax.ShapeDtypeStruct((rows, width), bf16),
        in_specs=in_vmem(len(parts)),
        out_specs=in_vmem(1)[0],
        compiler_params=pltpu.CompilerParams(vmem_limit_bytes=8 * MIB),
        cost_estimate=pl.CostEstimate(
            flops=0, bytes_accessed=4 * rows * width, transcendentals=0
        ),
    )(*parts)


def product(a, b):
    return jnp.dot(a, b, preferred_element_type=f32).astype(bf16)


def project(halves, weight, ids, jobs):
    used = sorted({half for _, half in jobs})

    def kernel(ids_ref, weight_ref, *refs):
        row_refs = dict(zip(used, refs))
        for (k, half), out_ref in zip(jobs, refs[len(used) :]):
            for j in (0, 2):
                pair = [
                    weight_ref[:, pl.ds(pl.multiple_of(ids_ref[4 * k + i] * 128, 128), 128)]
                    for i in (j, j + 1)
                ]
                out_ref[:, j * 128 : j * 128 + 256] = product(
                    row_refs[half][...], jnp.concatenate(pair, 1)
                )

    depth = weight.shape[0]
    return pl.pallas_call(
        kernel,
        out_shape=(jax.ShapeDtypeStruct((256, 512), bf16),) * len(jobs),
        in_specs=[pl.BlockSpec(memory_space=pltpu.SMEM)] + in_vmem(1 + len(used)),
        out_specs=tuple(in_vmem(len(jobs))),
        compiler_params=pltpu.CompilerParams(vmem_limit_bytes=16 * MIB),
        cost_estimate=pl.CostEstimate(
            flops=2 * len(jobs) * 256 * 512 * depth,
            bytes_accessed=len(jobs) * 1024 * depth,
            transcendentals=0,
        ),
    )(ids, weight, *[halves[half] for half in used])


def relay(move, add, halves):
    (first_a, first_b), (second_a, second_b), (third_a, third_b) = halves
    moved_a, moved_b = move(second_a, 3), move(second_b, 1)
    below_b, above_a = move(first_b, 3), move(third_a, 1)
    below_a, above_b = move(add(first_a, moved_a), 3), move(add(third_b, moved_b), 1)
    return below_a, below_b, above_a, above_b


def add_kernel(a_ref, b_ref, out_ref):
    out_ref[...] = total_of([a_ref[...], b_ref[...]]).astype(bf16)


def sum_kernel(own_a, own_b, below_a, below_b, above_a, above_b, *out_refs):
    for j, out_ref in enumerate(out_refs):
        at = slice(j * 128, j * 128 + 128)
        for row, refs in ((0, (own_a, below_a, above_a)), (256, (own_b, below_b, above_b))):
            out_ref[row : row + 256] = total_of([ref[:, at] for ref in refs]).astype(out_ref.dtype)


def scatter_gy(halves, weight, ids):
    second_a, third_a = project(halves, weight, ids, ((2, 0), (3, 0)))
    second_b, first_b = project(halves, weight, ids, ((2, 1), (1, 1)))
    first_a, third_b = project(halves, weight, ids, ((1, 0), (3, 1)))
    own_a, own_b = project(halves, weight, ids, ((0, 0), (0, 1)))
    half = jax.ShapeDtypeStruct((256, 512), bf16)
    moved = relay(
        lambda a, d: from_ring(a, d, 0),
        lambda mine, other: local(add_kernel, half, mine, other),
        ((first_a, first_b), (second_a, second_b), (third_a, third_b)),
    )
    part, own = (jax.ShapeDtypeStruct((512, 128), dtype) for dtype in (bf16, f32))
    sums = local(sum_kernel, (own, part, part, part), own_a, own_b, *moved)
    return [sums[0]] + [from_ring(sums[j], (4 - j) % 4, 1) for j in (1, 3, 2)]


def gather_gy(rows):
    first = [from_ring(rows, k, 0) for k in (1, 3, 2)]
    first = stack([rows, first[0], first[2], first[1]])
    last = [from_ring(first, k, 1) for k in (1, 3, 2)]
    return [first, last[0], last[2], last[1]]


def scale_kernel(
    ids_ref, s0_ref, s1_ref, s2_ref, s3_ref, gain_ref, same_ref, other_ref, square_ref
):
    squares = jnp.zeros((512, 128), f32)
    for k, stack_ref in enumerate((s0_ref, s1_ref, s2_ref, s3_ref)):
        for j in range(4):
            chunk = ids_ref[4 * j + k]
            wide = stack_ref[j * 512 : j * 512 + 512].astype(f32)
            squares = squares + wide * wide
            scaled = (wide * gain_ref[pl.ds(chunk, 1), :]).astype(bf16)
            at = pl.ds(pl.multiple_of(chunk * 128, 128), 128)
            same_ref[:, at] = scaled[:256]
            other_ref[:, at] = scaled[256:]
    square = jnp.sum(squares, axis=1, keepdims=True)
    high = square.astype(bf16).astype(f32)
    low = (square - high).astype(bf16).astype(f32)
    lane = lax.broadcasted_iota(jnp.int32, (512, 128), 1)
    square_ref[...] = jnp.where(lane == 0, high, jnp.where(lane == 1, low, 0.0)).astype(bf16)


def scale_features(stacks, gain, ids):
    return pl.pallas_call(
        scale_kernel,
        out_shape=(
            jax.ShapeDtypeStruct((256, 2048), bf16),
            jax.ShapeDtypeStruct((256, 2048), bf16),
            jax.ShapeDtypeStruct((512, 128), bf16),
        ),
        in_specs=[pl.BlockSpec(memory_space=pltpu.SMEM)] + in_vmem(5),
        out_specs=tuple(in_vmem(3)),
        compiler_params=pltpu.CompilerParams(vmem_limit_bytes=8 * MIB),
        cost_estimate=pl.CostEstimate(flops=2**33, bytes_accessed=2**25, transcendentals=0),
    )(ids, *stacks, gain)


def high_and_low(square):
    square = jnp.sum(square, axis=1, keepdims=True)
    high = square.astype(bf16).astype(f32)
    lane = lax.broadcasted_iota(jnp.int32, (square.shape[0], 128), 1)
    return jnp.where(lane == 0, high, jnp.where(lane == 1, square - high, 0.0))


def pair_kernel(gate_ref, up_ref, square_ref, moved_gate_ref, moved_up_ref, *out_refs):
    row = 0
    for out_ref in out_refs:
        at = slice(row, row + out_ref.shape[0])
        row += out_ref.shape[0]
        gate = gate_ref[at, :].astype(f32) + moved_gate_ref[at, :].astype(f32)
        up = up_ref[at, :].astype(f32) + moved_up_ref[at, :1664].astype(f32)
        square = square_ref[at, :].astype(f32) + moved_up_ref[at, 1664:].astype(f32)
        out_ref[:, :1664] = gate.astype(out_ref.dtype)
        out_ref[:, 1664:3328] = up.astype(out_ref.dtype)
        out_ref[:, 3328:] = high_and_low(square).astype(out_ref.dtype)


def relay_kernel(mine_ref, moved_ref, out_ref):
    out_ref[:, :3328] = (
        mine_ref[:, :3328].astype(f32) + moved_ref[:, :3328].astype(f32)
    ).astype(bf16)
    square = mine_ref[:, 3328:].astype(f32) + moved_ref[:, 3328:].astype(f32)
    out_ref[:, 3328:] = high_and_low(square).astype(bf16)


def act_kernel(own_ref, a_ref, b_ref, c_ref, d_ref, out_ref):
    for rows, refs in ((slice(0, 32), (a_ref, c_ref)), (slice(32, 64), (b_ref, d_ref))):

        def total(at):
            return own_ref[rows, at] + refs[0][:, at].astype(f32) + refs[1][:, at].astype(f32)

        square = jnp.sum(total(slice(3328, 3456)), axis=1, keepdims=True)
        scale = lax.rsqrt(square / D + 1e-05)
        gate, up = total(slice(0, 1664)) * scale, total(slice(1664, 3328)) * scale
        out_ref[rows, :] = (gate / (1.0 + jnp.exp(-gate)) * up).astype(bf16)


def local(kernel, out_shape, *args):
    many = isinstance(out_shape, tuple)
    return pl.pallas_call(
        kernel,
        out_shape=out_shape,
        in_specs=in_vmem(len(args)),
        out_specs=tuple(in_vmem(len(out_shape))) if many else in_vmem(1)[0],
        compiler_params=pltpu.CompilerParams(vmem_limit_bytes=12 * MIB),
        cost_estimate=pl.CostEstimate(flops=2**22, bytes_accessed=2**22, transcendentals=0),
    )(*args)


def gather_gx(rows):
    same = [rows] + [from_y(rows, k) for k in (1, 3, 2)]
    same = stack([same[0], same[1], same[3], same[2]])
    return same, from_core(same)


def own_order_kernel(blocks_ref, hidden_ref, out_ref, turned_ref):
    turned_ref[...] = hidden_ref[...].astype(f32).T
    for m in range(8):
        at = pl.ds(pl.multiple_of(blocks_ref[m] * 64, 64), 64)
        out_ref[64 * m : 64 * m + 64] = turned_ref[at, :].astype(bf16)


def final_kernel(blocks_ref, resid_ref, a_ref, b_ref, c_ref, d_ref, out_ref, total_ref):
    total = total_of([ref[...] for ref in (resid_ref, a_ref, b_ref, c_ref, d_ref)])
    for m in range(8):
        at = pl.ds(pl.multiple_of(blocks_ref[m] * 64, 64), 64)
        total_ref[at, :] = total[64 * m : 64 * m + 64]
    out_ref[...] = total_ref[...].T.astype(bf16)


def reorder(kernel, shape, blocks, *args):
    return pl.pallas_call(
        kernel,
        out_shape=jax.ShapeDtypeStruct(shape, bf16),
        in_specs=[pl.BlockSpec(memory_space=pltpu.SMEM)] + in_vmem(len(args)),
        out_specs=in_vmem(1)[0],
        scratch_shapes=[pltpu.VMEM((512, 128), f32)],
        compiler_params=pltpu.CompilerParams(vmem_limit_bytes=4 * MIB),
        cost_estimate=pl.CostEstimate(flops=2**20, bytes_accessed=2**20, transcendentals=0),
    )(blocks, *args)


def per_device(
    hidden,
    queries,
    new_kv,
    key_cache,
    value_cache,
    lengths,
    out_weight,
    norm_gain,
    w_gate,
    w_up,
    w_down,
):
    gx, gy = lax.axis_index("gx"), lax.axis_index("gy")
    y, core, z, x = gx >> 1, gx & 1, gy >> 2, gy & 3
    up_k, up_j = jnp.arange(16, dtype=jnp.int32) >> 2, jnp.arange(16, dtype=jnp.int32) & 3
    ids = jnp.where(
        core == 0,
        ((z + up_j) & 3) * 4 + ((x + up_k) & 3),
        ((z + up_k) & 3) * 4 + ((x + up_j) & 3),
    )
    got = lax.all_to_all(pack(queries, new_kv, norm_gain), "gy", 0, 0, tiled=True)
    pair_rows = got[:, :, 512:576].transpose(1, 0, 2).reshape(4, 1024)
    gain = got[:, 0, 640:].astype(f32)
    attended = attend(got[:, :, :512].transpose(1, 0, 2), pair_rows, key_cache, value_cache, lengths)
    head_block = lax.all_to_all(attended, "gy", 1, 1, tiled=True)
    head_block = head_block.transpose(1, 0, 2).reshape(64, 512)
    heads = gather_gx(head_block)
    block = jnp.arange(8, dtype=jnp.int32)
    blocks = ((y + (block & 3)) & 3) * 2 + (core ^ (block >> 2))
    mine = reorder(own_order_kernel, (512, 128), blocks, hidden)
    resid = total_of([mine] + scatter_gy(heads, out_weight, ids)).astype(bf16)
    same, other, squares = scale_features(gather_gy(resid), gain, ids)

    gate_moved = from_core(product(other, w_gate))
    up_moved = from_core(jnp.concatenate([product(other, w_up), squares[256:]], 1))
    message = jax.ShapeDtypeStruct((32, 3456), bf16)
    own, *pairs = local(
        pair_kernel,
        (jax.ShapeDtypeStruct((64, 3456), f32),) + (message,) * 6,
        product(same, w_gate),
        product(same, w_up),
        squares[:256],
        gate_moved,
        up_moved,
    )
    moved = relay(
        from_y,
        lambda mine, other: local(relay_kernel, message, mine, other),
        (pairs[:2], pairs[2:4], pairs[4:]),
    )
    act = local(act_kernel, jax.ShapeDtypeStruct((64, 1664), bf16), own, *moved)
    return reorder(final_kernel, (128, 512), blocks, resid, *scatter_gy(gather_gx(act), w_down, ids))


def solution(mesh):
    return jax.shard_map(
        per_device,
        mesh=mesh,
        in_specs=(
            P(("gx", "gy"), None),
            P("gx", "gy"),
            P("gx", "gy"),
            P(("gx", "gy"), None, None),
            P(("gx", "gy"), None, None),
            P(("gx", "gy")),
            P("gy", "gx"),
            P(("gx", "gy")),
            P("gx", "gy"),
            P("gx", "gy"),
            P("gy", "gx"),
        ),
        out_specs=P(("gx", "gy"), None),
        check_vma=False,
    )
```

```python
import jax
import jax.numpy as jnp
from jax import lax
from jax.experimental import pallas as pl
from jax.experimental.pallas import tpu as pltpu
from jax.sharding import PartitionSpec as P

D = 16384
HQ = 64
HK = 4
HD = 128
bf16 = jnp.bfloat16
f32 = jnp.float32
MIB = 1024 * 1024


def from_y(a, d):
    return lax.ppermute(a, "gx", [(i, ((i // 2 - d) % 4) * 2 + i % 2) for i in range(8)])


def from_core(a):
    return lax.ppermute(a, "gx", [(i, i ^ 1) for i in range(8)])


def from_ring(a, d, leg):
    pairs = []
    for gx in range(8):
        for gy in range(16):
            z, x = gy // 4, gy % 4
            if gx % 2 == leg:
                x = (x - d) % 4
            else:
                z = (z - d) % 4
            pairs.append((gx * 16 + gy, gx * 16 + z * 4 + x))
    return lax.ppermute(a, ("gx", "gy"), pairs)


def total_of(parts):
    out = parts[0].astype(f32)
    for part in parts[1:]:
        out = out + part.astype(f32)
    return out


def pack_kernel(query_ref, pair_ref, gain_ref, out_ref):
    query, pair = query_ref[...].astype(f32), pair_ref[...].astype(f32)
    gain = jnp.broadcast_to(gain_ref[...].astype(f32), (4, 128))
    for s in range(16):
        out_ref[s, :, :512] = query[4 * s : 4 * s + 4].astype(bf16)
        out_ref[s, :, 512:576] = pair[4 * s : 4 * s + 4].astype(bf16)
        out_ref[s, :, 640:] = gain.astype(bf16)


def pack(queries, new_kv, gain):
    return pl.pallas_call(
        pack_kernel,
        out_shape=jax.ShapeDtypeStruct((16, 4, 768), bf16),
        compiler_params=pltpu.CompilerParams(vmem_limit_bytes=4 * MIB),
        cost_estimate=pl.CostEstimate(flops=2**35, bytes_accessed=2**24, transcendentals=0),
    )(queries, new_kv, gain.reshape(1, 128))


def attend_kernel(lengths_ref, got_ref, pair_ref, key_ref, value_ref, out_ref):
    group = (lax.broadcasted_iota(jnp.int32, (64, 1), 0) % 16) // 4
    score_scale = 1.0 / HD**0.5
    for beam in range(4):
        got = got_ref[beam]
        query = jnp.concatenate([got[:, i * 128 : i * 128 + 128] for i in range(4)], 0)
        zero = jnp.zeros_like(query)
        wide = jnp.concatenate([jnp.where(group == g, query, zero) for g in range(4)], 1)
        pair = pair_ref[beam : beam + 1].astype(f32)
        scores = lax.dot_general(
            wide, key_ref[beam], (((1,), (1,)), ((), ())), preferred_element_type=f32
        )
        live = lax.broadcasted_iota(jnp.int32, scores.shape, 1) < lengths_ref[beam]
        scores = jnp.where(live, scores * score_scale, -jnp.inf)
        self_score = jnp.sum(wide.astype(f32) * pair[:, :512], axis=1, keepdims=True) * score_scale
        peak = jnp.maximum(jnp.max(scores, axis=1, keepdims=True), self_score)
        raw_weights = jnp.exp(scores - peak)
        self_weight = jnp.exp(self_score - peak)
        total = jnp.sum(raw_weights, axis=1, keepdims=True) + self_weight
        probs = (raw_weights / total).astype(bf16)
        own_prob = (self_weight / total).astype(bf16).astype(f32)
        mixed = jnp.dot(probs, value_ref[beam], preferred_element_type=f32)
        mixed = mixed + own_prob * pair[:, 512:]
        out = jnp.zeros((64, 128), f32)
        for g in range(4):
            out = out + jnp.where(group == g, mixed[:, g * 128 : g * 128 + 128], 0.0)
        out = out.astype(bf16)
        for i in range(4):
            out_ref[beam, :, i * 128 : i * 128 + 128] = out[i * 16 : i * 16 + 16]


def in_vmem(count):
    return [pl.BlockSpec(memory_space=pltpu.VMEM)] * count


def attend(got, pair, key_cache, value_cache, lengths):
    return pl.pallas_call(
        attend_kernel,
        out_shape=jax.ShapeDtypeStruct((4, 16, 512), bf16),
        in_specs=[pl.BlockSpec(memory_space=pltpu.SMEM)] + in_vmem(4),
        out_specs=in_vmem(1)[0],
        compiler_params=pltpu.CompilerParams(vmem_limit_bytes=8 * MIB),
        cost_estimate=pl.CostEstimate(flops=10**8, bytes_accessed=2**21, transcendentals=65536),
    )(lengths, got, pair, key_cache, value_cache)


def stack_kernel(*refs):
    row = 0
    for ref in refs[:-1]:
        refs[-1][row : row + ref.shape[0]] = ref[...]
        row += ref.shape[0]


def stack(parts):
    rows, width = sum(part.shape[0] for part in parts), parts[0].shape[1]
    return pl.pallas_call(
        stack_kernel,
        out_shape=jax.ShapeDtypeStruct((rows, width), bf16),
        in_specs=in_vmem(len(parts)),
        out_specs=in_vmem(1)[0],
        compiler_params=pltpu.CompilerParams(vmem_limit_bytes=8 * MIB),
        cost_estimate=pl.CostEstimate(
            flops=0, bytes_accessed=4 * rows * width, transcendentals=0
        ),
    )(*parts)


def product(a, b):
    return jnp.dot(a, b, preferred_element_type=f32).astype(bf16)


def project(halves, weight, ids, jobs):
    used = sorted({half for _, half in jobs})

    def kernel(ids_ref, weight_ref, *refs):
        row_refs = dict(zip(used, refs))
        for (k, half), out_ref in zip(jobs, refs[len(used) :]):
            for j in (0, 2):
                pair = [
                    weight_ref[:, pl.ds(pl.multiple_of(ids_ref[4 * k + i] * 128, 128), 128)]
                    for i in (j, j + 1)
                ]
                out_ref[:, j * 128 : j * 128 + 256] = product(
                    row_refs[half][...], jnp.concatenate(pair, 1)
                )

    depth = weight.shape[0]
    return pl.pallas_call(
        kernel,
        out_shape=(jax.ShapeDtypeStruct((256, 512), bf16),) * len(jobs),
        in_specs=[pl.BlockSpec(memory_space=pltpu.SMEM)] + in_vmem(1 + len(used)),
        out_specs=tuple(in_vmem(len(jobs))),
        compiler_params=pltpu.CompilerParams(vmem_limit_bytes=16 * MIB),
        cost_estimate=pl.CostEstimate(
            flops=2 * len(jobs) * 256 * 512 * depth,
            bytes_accessed=len(jobs) * 1024 * depth,
            transcendentals=0,
        ),
    )(ids, weight, *[halves[half] for half in used])


def relay(move, add, halves):
    (first_a, first_b), (second_a, second_b), (third_a, third_b) = halves
    moved_a, moved_b = move(second_a, 3), move(second_b, 1)
    below_b, above_a = move(first_b, 3), move(third_a, 1)
    below_a, above_b = move(add(first_a, moved_a), 3), move(add(third_b, moved_b), 1)
    return below_a, below_b, above_a, above_b


def add_kernel(a_ref, b_ref, out_ref):
    out_ref[...] = total_of([a_ref[...], b_ref[...]]).astype(bf16)


def sum_kernel(own_a, own_b, below_a, below_b, above_a, above_b, *out_refs):
    for j, out_ref in enumerate(out_refs):
        at = slice(j * 128, j * 128 + 128)
        for row, refs in ((0, (own_a, below_a, above_a)), (256, (own_b, below_b, above_b))):
            out_ref[row : row + 256] = total_of([ref[:, at] for ref in refs]).astype(out_ref.dtype)


def scatter_gy(halves, weight, ids):
    (second_a,) = project(halves, weight, ids, ((2, 0),))
    third_a, second_b = project(halves, weight, ids, ((3, 0), (2, 1)))
    first_b, first_a = project(halves, weight, ids, ((1, 1), (1, 0)))
    third_b, own_a, own_b = project(halves, weight, ids, ((3, 1), (0, 0), (0, 1)))
    half = jax.ShapeDtypeStruct((256, 512), bf16)
    moved = relay(
        lambda a, d: from_ring(a, d, 0),
        lambda mine, other: local(add_kernel, half, mine, other),
        ((first_a, first_b), (second_a, second_b), (third_a, third_b)),
    )
    part, own = (jax.ShapeDtypeStruct((512, 128), dtype) for dtype in (bf16, f32))
    sums = local(sum_kernel, (own, part, part, part), own_a, own_b, *moved)
    return [sums[0]] + [from_ring(sums[j], (4 - j) % 4, 1) for j in (1, 3, 2)]


def gather_gy(rows):
    first = [from_ring(rows, k, 0) for k in (1, 3, 2)]
    first = stack([rows, first[0], first[2], first[1]])
    last = [from_ring(first, k, 1) for k in (1, 3, 2)]
    return [first, last[0], last[2], last[1]]


def scale_kernel(
    ids_ref, s0_ref, s1_ref, s2_ref, s3_ref, gain_ref, same_ref, other_ref, square_ref
):
    squares = jnp.zeros((512, 128), f32)
    for k, stack_ref in enumerate((s0_ref, s1_ref, s2_ref, s3_ref)):
        for j in range(4):
            chunk = ids_ref[4 * j + k]
            wide = stack_ref[j * 512 : j * 512 + 512].astype(f32)
            squares = squares + wide * wide
            scaled = (wide * gain_ref[pl.ds(chunk, 1), :]).astype(bf16)
            at = pl.ds(pl.multiple_of(chunk * 128, 128), 128)
            same_ref[:, at] = scaled[:256]
            other_ref[:, at] = scaled[256:]
    square = jnp.sum(squares, axis=1, keepdims=True)
    high = square.astype(bf16).astype(f32)
    low = (square - high).astype(bf16).astype(f32)
    lane = lax.broadcasted_iota(jnp.int32, (512, 128), 1)
    square_ref[...] = jnp.where(lane == 0, high, jnp.where(lane == 1, low, 0.0)).astype(bf16)


def scale_features(stacks, gain, ids):
    return pl.pallas_call(
        scale_kernel,
        out_shape=(
            jax.ShapeDtypeStruct((256, 2048), bf16),
            jax.ShapeDtypeStruct((256, 2048), bf16),
            jax.ShapeDtypeStruct((512, 128), bf16),
        ),
        in_specs=[pl.BlockSpec(memory_space=pltpu.SMEM)] + in_vmem(5),
        out_specs=tuple(in_vmem(3)),
        compiler_params=pltpu.CompilerParams(vmem_limit_bytes=8 * MIB),
        cost_estimate=pl.CostEstimate(flops=2**33, bytes_accessed=2**25, transcendentals=0),
    )(ids, *stacks, gain)


def high_and_low(square):
    square = jnp.sum(square, axis=1, keepdims=True)
    high = square.astype(bf16).astype(f32)
    lane = lax.broadcasted_iota(jnp.int32, (square.shape[0], 128), 1)
    return jnp.where(lane == 0, high, jnp.where(lane == 1, square - high, 0.0))


def pair_kernel(gate_ref, up_ref, square_ref, moved_gate_ref, moved_up_ref, *out_refs):
    row = 0
    for out_ref in out_refs:
        at = slice(row, row + out_ref.shape[0])
        row += out_ref.shape[0]
        gate = gate_ref[at, :].astype(f32) + moved_gate_ref[at, :].astype(f32)
        up = up_ref[at, :].astype(f32) + moved_up_ref[at, :1664].astype(f32)
        square = square_ref[at, :].astype(f32) + moved_up_ref[at, 1664:].astype(f32)
        out_ref[:, :1664] = gate.astype(out_ref.dtype)
        out_ref[:, 1664:3328] = up.astype(out_ref.dtype)
        out_ref[:, 3328:] = high_and_low(square).astype(out_ref.dtype)


def relay_kernel(mine_ref, moved_ref, out_ref):
    out_ref[:, :3328] = (
        mine_ref[:, :3328].astype(f32) + moved_ref[:, :3328].astype(f32)
    ).astype(bf16)
    square = mine_ref[:, 3328:].astype(f32) + moved_ref[:, 3328:].astype(f32)
    out_ref[:, 3328:] = high_and_low(square).astype(bf16)


def act_kernel(own_ref, a_ref, b_ref, c_ref, d_ref, out_ref):
    for rows, refs in ((slice(0, 32), (a_ref, c_ref)), (slice(32, 64), (b_ref, d_ref))):

        def total(at):
            return own_ref[rows, at] + refs[0][:, at].astype(f32) + refs[1][:, at].astype(f32)

        square = jnp.sum(total(slice(3328, 3456)), axis=1, keepdims=True)
        scale = lax.rsqrt(square / D + 1e-05)
        gate, up = total(slice(0, 1664)) * scale, total(slice(1664, 3328)) * scale
        out_ref[rows, :] = (gate / (1.0 + jnp.exp(-gate)) * up).astype(bf16)


def local(kernel, out_shape, *args):
    many = isinstance(out_shape, tuple)
    return pl.pallas_call(
        kernel,
        out_shape=out_shape,
        in_specs=in_vmem(len(args)),
        out_specs=tuple(in_vmem(len(out_shape))) if many else in_vmem(1)[0],
        compiler_params=pltpu.CompilerParams(vmem_limit_bytes=12 * MIB),
        cost_estimate=pl.CostEstimate(flops=2**22, bytes_accessed=2**22, transcendentals=0),
    )(*args)


def gather_gx(rows):
    same = [rows] + [from_y(rows, k) for k in (1, 3, 2)]
    same = stack([same[0], same[1], same[3], same[2]])
    return same, from_core(same)


def own_order_kernel(blocks_ref, hidden_ref, out_ref, turned_ref):
    turned_ref[...] = hidden_ref[...].astype(f32).T
    for m in range(8):
        at = pl.ds(pl.multiple_of(blocks_ref[m] * 64, 64), 64)
        out_ref[64 * m : 64 * m + 64] = turned_ref[at, :].astype(bf16)


def final_kernel(blocks_ref, resid_ref, a_ref, b_ref, c_ref, d_ref, out_ref, total_ref):
    total = total_of([ref[...] for ref in (resid_ref, a_ref, b_ref, c_ref, d_ref)])
    for m in range(8):
        at = pl.ds(pl.multiple_of(blocks_ref[m] * 64, 64), 64)
        total_ref[at, :] = total[64 * m : 64 * m + 64]
    out_ref[...] = total_ref[...].T.astype(bf16)


def reorder(kernel, shape, blocks, *args):
    return pl.pallas_call(
        kernel,
        out_shape=jax.ShapeDtypeStruct(shape, bf16),
        in_specs=[pl.BlockSpec(memory_space=pltpu.SMEM)] + in_vmem(len(args)),
        out_specs=in_vmem(1)[0],
        scratch_shapes=[pltpu.VMEM((512, 128), f32)],
        compiler_params=pltpu.CompilerParams(vmem_limit_bytes=4 * MIB),
        cost_estimate=pl.CostEstimate(flops=2**20, bytes_accessed=2**20, transcendentals=0),
    )(blocks, *args)


def per_device(
    hidden,
    queries,
    new_kv,
    key_cache,
    value_cache,
    lengths,
    out_weight,
    norm_gain,
    w_gate,
    w_up,
    w_down,
):
    gx, gy = lax.axis_index("gx"), lax.axis_index("gy")
    y, core, z, x = gx >> 1, gx & 1, gy >> 2, gy & 3
    up_k, up_j = jnp.arange(16, dtype=jnp.int32) >> 2, jnp.arange(16, dtype=jnp.int32) & 3
    ids = jnp.where(
        core == 0,
        ((z + up_j) & 3) * 4 + ((x + up_k) & 3),
        ((z + up_k) & 3) * 4 + ((x + up_j) & 3),
    )
    got = lax.all_to_all(pack(queries, new_kv, norm_gain), "gy", 0, 0, tiled=True)
    pair_rows = got[:, :, 512:576].transpose(1, 0, 2).reshape(4, 1024)
    gain = got[:, 0, 640:].astype(f32)
    attended = attend(got[:, :, :512].transpose(1, 0, 2), pair_rows, key_cache, value_cache, lengths)
    head_block = lax.all_to_all(attended, "gy", 1, 1, tiled=True)
    head_block = head_block.transpose(1, 0, 2).reshape(64, 512)
    heads = gather_gx(head_block)
    block = jnp.arange(8, dtype=jnp.int32)
    blocks = ((y + (block & 3)) & 3) * 2 + (core ^ (block >> 2))
    mine = reorder(own_order_kernel, (512, 128), blocks, hidden)
    resid = total_of([mine] + scatter_gy(heads, out_weight, ids)).astype(bf16)
    same, other, squares = scale_features(gather_gy(resid), gain, ids)

    gate_moved = from_core(product(other, w_gate))
    up_moved = from_core(jnp.concatenate([product(other, w_up), squares[256:]], 1))
    message = jax.ShapeDtypeStruct((32, 3456), bf16)
    own, *pairs = local(
        pair_kernel,
        (jax.ShapeDtypeStruct((64, 3456), f32),) + (message,) * 6,
        product(same, w_gate),
        product(same, w_up),
        squares[:256],
        gate_moved,
        up_moved,
    )
    moved = relay(
        from_y,
        lambda mine, other: local(relay_kernel, message, mine, other),
        (pairs[:2], pairs[2:4], pairs[4:]),
    )
    act = local(act_kernel, jax.ShapeDtypeStruct((64, 1664), bf16), own, *moved)
    return reorder(final_kernel, (128, 512), blocks, resid, *scatter_gy(gather_gx(act), w_down, ids))


def solution(mesh):
    return jax.shard_map(
        per_device,
        mesh=mesh,
        in_specs=(
            P(("gx", "gy"), None),
            P("gx", "gy"),
            P("gx", "gy"),
            P(("gx", "gy"), None, None),
            P(("gx", "gy"), None, None),
            P(("gx", "gy")),
            P("gy", "gx"),
            P(("gx", "gy")),
            P("gx", "gy"),
            P("gx", "gy"),
            P("gy", "gx"),
        ),
        out_specs=P(("gx", "gy"), None),
        check_vma=False,
    )
```
